128 devices in a mesh: dom: 64 (over x, z, y), rhs: 2 (over core).
Axes of the slice: x: 4, y: 4, z: 4, core: 2. Of those that a mesh axis runs over, the one named last changes fastest.
Arguments:
- adjoint: bfloat16 [1024, 64, 320], P('dom', 'rhs'), may hold values from -6 to 6
- adj_rhs: float32 [1024, 64, 320], P('dom', 'rhs'), may hold values from -6 to 6
- diag_inv: bfloat16 [1024, 320, 320], P('dom'), may hold values from -0.3125 to 0.3125
- diag_jac: bfloat16 [1024, 320, 320], P('dom'), may hold values from -0.3125 to 0.3125
- upper: bfloat16 [1024, 4, 320, 320], P('dom', 'rhs'), may hold values from -0.25 to 0.25
- face_jac: bfloat16 [1024, 4, 320, 320], P('dom', 'rhs'), may hold values from -0.25 to 0.25
- face_ref: int32 [1024, 4], P('dom'), may hold values from 0 to 79, as said below
- send_list: int32 [64, 64, 1], P('dom'), may hold values from 0 to 15
- colour: int32 [1024], P('dom'), may hold values from 0 to 3, as said below
Outputs:
- adjoint_new: bfloat16 [1024, 64, 320], P('dom', 'rhs')
- residual: float32 [1024, 64, 320], P('dom', 'rhs')
The draws below stay inside these ranges and needn't reach their ends.
Inputs may be any that keep to these rules, and one draw needn't show every extreme that they name: `face_ref`: for an element of partition d, a value below 16 names another of d's own elements; a value 16 + 1 * q + s with 0 <= s < 1 names the element that partition q lists in send_list[q, d, s]. Each partition reads from exactly 32 other partitions, and each of their 1 slots is named by exactly one face of the partition; other slots are never named. Each partition has between 1 and 8 elements of colour 0, and some partition has exactly 8.
All inputs are finite; a program needn't handle non-finite values.
Results may differ from the reference program's by a relative error of at most 0.0034.
Values may be sent and summed in bfloat16 or wider, within the bound.
No kernel may reach another device: no remote copies, remote signals or barrier semaphores. Data moves between devices by JAX's collectives and lax.ppermute only.
A program may use at most 128 MiB of HBM per device.

```python
import jax
import jax.numpy as jnp
from jax import lax

NB = 320
RHS = 64
E_DEV = 16
FACES = 4
SLOTS = 1
NCOL = 4
PEERS = 32
CMAX = 8
PARTS_SIZE = 64
ELEMS = 1024


def draw_face_ref(key, part):
    key = jax.random.fold_in(key, 11)
    keys = jax.random.split(key, PARTS_SIZE)

    def one_part(owner, subkey):
        key_one, key_two, key_three = jax.random.split(subkey, 3)
        shuffled = jax.random.permutation(key_one, PARTS_SIZE - 1)
        rotated = (shuffled + (PARTS_SIZE - 2 - shuffled[0])) % (PARTS_SIZE - 1)
        shuffled = jnp.where(owner == 0, rotated, shuffled)
        offsets = shuffled[:PEERS] + 1
        sources = (owner + offsets) % PARTS_SIZE
        remote_ids = (E_DEV + sources[:, None] * SLOTS + jnp.arange(SLOTS)[None, :]).reshape(-1)
        steps_away = jax.random.randint(key_two, (E_DEV, FACES), 1, E_DEV)
        steps_away = steps_away.at[1, 0].set(E_DEV - 1)
        local_ids = (jnp.arange(E_DEV)[:, None] + steps_away) % E_DEV
        places = jax.random.permutation(key_three, E_DEV * FACES - 1)[:PEERS * SLOTS]
        places = jnp.where(places >= FACES, places + 1, places)
        return local_ids.reshape(-1).at[places].set(remote_ids).reshape(E_DEV, FACES)
    return jax.vmap(one_part)(jnp.arange(PARTS_SIZE), keys).reshape(ELEMS, FACES).astype(jnp.int32)


def draw_colour(key, part):
    key = jax.random.fold_in(key, 23)
    key_busy, key_rest = jax.random.split(key)
    busiest = jax.random.randint(key_busy, (), 0, PARTS_SIZE)
    keys = jax.random.split(key_rest, PARTS_SIZE)

    def one_part(owner, subkey):
        key_one, key_two, key_three = jax.random.split(subkey, 3)
        number = jax.random.randint(key_one, (), 1, CMAX + 1)
        number = jnp.where(owner == busiest, CMAX, number)
        order = jax.random.permutation(key_two, E_DEV)
        others = jax.random.randint(key_three, (E_DEV,), 1, NCOL)
        return jnp.where(order < number, 0, others)
    return jax.vmap(one_part)(jnp.arange(PARTS_SIZE), keys).reshape(ELEMS).astype(jnp.int32)


def with_ends(entries, own_key, low, top_value):
    longest = entries.shape.index(max(entries.shape))
    spots = []
    for shift in (0, 1):
        where = [jax.random.randint(jax.random.fold_in(own_key, axis), (), 0, length) for axis, length in enumerate(entries.shape)]
        where[longest] = (where[longest] + shift) % entries.shape[longest]
        spots.append(tuple(where))
    return entries.at[spots[0]].set(low).at[spots[1]].set(top_value)


def level_of(rng, dims, pieces, smallest, largest):
    level = 1.0
    for axis_at, shards_of in pieces:
        draws = jax.random.uniform(jax.random.fold_in(jax.random.fold_in(rng, 6), axis_at), (shards_of,), jnp.float32, smallest / len(pieces), largest / len(pieces))
        level = level * jnp.repeat(jnp.exp(draws), dims[axis_at] // shards_of).reshape((-1,) + (1,) * (len(dims) - 1 - axis_at))
    return level


def noise(rng, shape, width, reach, pieces=(), kind=jnp.bfloat16):
    factor_of = level_of(rng, shape, pieces, -0.22, 0.18) if pieces else 1.0
    values = jax.random.normal(rng, shape, jnp.float32) * width * factor_of
    return jnp.minimum(jnp.maximum(values, -reach), reach).astype(kind)


def setup_inputs(seed: int = 0) -> dict:
    splits = jax.random.split(jax.random.key(seed), 10)
    adjoint = noise(splits[0], (ELEMS, RHS, NB), 1.0, 6.0, ((0, 64), (1, 2)))
    adj_rhs = noise(splits[1], (ELEMS, RHS, NB), 1.0, 6.0, ((0, 64), (1, 2)), jnp.float32)
    diag_inv = noise(splits[2], (ELEMS, NB, NB), NB ** -0.5, 0.3125, ((0, 64),))
    diag_jac = noise(splits[3], (ELEMS, NB, NB), NB ** -0.5, 0.3125, ((0, 64),))
    upper = noise(splits[4], (ELEMS, FACES, NB, NB), (2 * NB) ** -0.5, 0.25, ((0, 64), (1, 2)))
    face_jac = noise(splits[5], (ELEMS, FACES, NB, NB), (2 * NB) ** -0.5, 0.25, ((0, 64), (1, 2)))
    face_ref = draw_face_ref(jax.random.fold_in(splits[9], 71), 0)
    send_list = with_ends(jax.random.randint(splits[7], (PARTS_SIZE, PARTS_SIZE, SLOTS), 0, E_DEV), jax.random.fold_in(splits[7], 1), 0, E_DEV - 1).astype(jnp.int32)
    colour = draw_colour(jax.random.fold_in(splits[9], 71), 0)
    return dict(adjoint=adjoint, adj_rhs=adj_rhs, diag_inv=diag_inv, diag_jac=diag_jac, upper=upper, face_jac=face_jac, face_ref=face_ref, send_list=send_list, colour=colour)


def reference(adjoint, adj_rhs, diag_inv, diag_jac, upper, face_jac, face_ref, send_list, colour):
    owner = (jnp.arange(ELEMS, dtype=jnp.int32) // E_DEV)[:, None]
    remote_slot = jnp.maximum(face_ref - E_DEV, 0)
    source = remote_slot // SLOTS
    slot_index = remote_slot % SLOTS
    remote_global = source * E_DEV + send_list[source, owner, slot_index]
    global_ref = jnp.where(face_ref >= E_DEV, remote_global, owner * E_DEV + face_ref).astype(jnp.int32)

    def shaped(array):
        return array.reshape((PARTS_SIZE, E_DEV) + array.shape[1:])

    def sweep_block(items):
        refs, rhs_block, inv_block, up_block, old_block, colour_block = items
        neighbours = adjoint[refs].astype(jnp.float32)
        pushed = jnp.einsum("efrn,efnm->erm", neighbours, up_block.astype(jnp.float32))
        reduced = (rhs_block - pushed).astype(jnp.bfloat16)
        swept_rows = jnp.einsum("ern,enm->erm", reduced.astype(jnp.float32), inv_block.astype(jnp.float32)).astype(jnp.bfloat16)
        return jnp.where((colour_block == 0)[:, None, None], swept_rows, old_block)

    updated = lax.map(sweep_block, (shaped(global_ref), shaped(adj_rhs), shaped(diag_inv), shaped(upper), shaped(adjoint), shaped(colour)))
    updated = updated.reshape(adjoint.shape)
    ext_rows = E_DEV + PARTS_SIZE * SLOTS

    def apply_block(carried, items):
        index, psi_block, jac_block, ref_block = items
        partial_value = jnp.einsum("ern,efnm->efrm", psi_block.astype(jnp.float32), jac_block.astype(jnp.float32))
        face_sums = jax.ops.segment_sum(partial_value.reshape((E_DEV * FACES, RHS, NB)), ref_block.reshape(-1), num_segments=ext_rows)
        rounded = lax.optimization_barrier(face_sums[E_DEV:].astype(jnp.bfloat16)).astype(jnp.float32)
        targets = (jnp.arange(PARTS_SIZE, dtype=jnp.int32)[:, None] * E_DEV + send_list[:, index, :]).reshape(-1)
        offset = (index * E_DEV).astype(jnp.int32)
        own_rows = lax.dynamic_slice_in_dim(carried, offset, E_DEV, 0) + face_sums[:E_DEV]
        carried = lax.dynamic_update_slice_in_dim(carried, own_rows, offset, 0)
        carried = carried.at[targets].add(rounded)
        return carried, None

    start_sums = jnp.zeros((ELEMS, RHS, NB), jnp.float32)
    scanned, unused = lax.scan(apply_block, start_sums, (jnp.arange(PARTS_SIZE, dtype=jnp.int32), shaped(updated), shaped(face_jac), shaped(face_ref)))
    applied = jnp.einsum("ern,enm->erm", updated.astype(jnp.float32), diag_jac.astype(jnp.float32)) + scanned
    return updated, adj_rhs - applied
```

```python
import jax
import jax.numpy as jnp
from jax import lax
from jax.experimental import pallas as pl
from jax.experimental.pallas import tpu as pltpu
from jax.sharding import PartitionSpec as P

N_EL, N_FACE, N_PART, C_MAX = 16, 4, 64, 8
R, N = 32, 320
MIB = 2**20

REF, SEND, COL, CORE = 0, 64, 128, 144

SMEM = pl.BlockSpec(memory_space=pltpu.SMEM)
VMEM = pl.BlockSpec(memory_space=pltpu.VMEM)
ANY = pl.BlockSpec(memory_space=pl.ANY)


def dot(a, b):
    return jnp.dot(a, b, preferred_element_type=jnp.float32)


def pack(v):
    tail = jnp.concatenate([v[:16, 256:], v[16:, 256:]], axis=1)
    return jnp.concatenate([v[:, :128], v[:, 128:256], tail], axis=0)


def unpack(p):
    tail = jnp.concatenate([p[64:, :64], p[64:, 64:]], axis=0)
    return jnp.concatenate([p[:32], p[32:64], tail], axis=1)


def order_by_colour(meta, order):
    def place(e, carry):
        zeros, others = carry
        is_zero = meta[COL + e] == 0
        order[jnp.where(is_zero, zeros, 15 - others)] = e
        step = is_zero.astype(jnp.int32)
        return zeros + step, others + 1 - step

    return lax.fori_loop(0, N_EL, place, (jnp.int32(0), jnp.int32(0)))[0]


def pack_kernel(meta, adj, out, packed):
    for e in range(N_EL):
        packed[e] = pack(adj[e])

    @pl.loop(0, N_PART, unroll=4)
    def _(q):
        out[q] = packed[meta[SEND + q]]


def select_kernel(meta, upper, out, order, sems):
    order_by_colour(meta, order)

    def copy(s):
        return pltpu.make_async_copy(upper.at[order[s]], out.at[s], sems.at[s])

    for s in range(C_MAX):
        copy(s).start()
    for s in range(C_MAX):
        copy(s).wait()


def face_copies(core, own_ref, own_at, other_ref, other_at, buf, slot, sem):
    own = pltpu.make_async_copy(
        own_ref.at[own_at], buf.at[slot, pl.ds(2 * core, 2)], sem.at[slot, 0]
    )
    other = pltpu.make_async_copy(
        other_ref.at[other_at], buf.at[slot, pl.ds(2 - 2 * core, 2)], sem.at[slot, 1]
    )
    return own, other


def faces_of(meta, e, x, weights, slot, send, local):
    for f in range(N_FACE):
        ref = meta[REF + e * N_FACE + f]
        product = dot(x, weights[slot, f])
        send[jnp.where(ref >= N_EL, ref - N_EL, N_PART)] = pack(product.astype(jnp.bfloat16))
        row = jnp.minimum(ref, N_EL)
        local[row] += product


def early_kernel(meta, adj, fj_own, fj_other, send_out, local_out, order, send, local, buf, sem):
    core = meta[CORE]
    count = order_by_colour(meta, order)

    def copies(s):
        e = order[s]
        return face_copies(core, fj_own, e, fj_other, e, buf, s, sem)

    @pl.loop(count, N_EL)
    def _(s):
        for c in copies(s):
            c.start()

    send[...] = jnp.zeros_like(send)
    local[...] = jnp.zeros_like(local)

    @pl.loop(count, N_EL)
    def _(s):
        for c in copies(s):
            c.wait()
        e = order[s]
        faces_of(meta, e, adj[e], buf, s, send, local)

    send_out[...] = send[:N_PART]
    local_out[...] = local[:N_EL]


def sweep_kernel(
    meta, adj, rhs, recv, send_in, local_in, upper, upper_other, dinv, fj_own, fj_other,
    new_out, send_out, local_out,
    order, send, local, red, new, up_buf, dinv_buf, fj_buf, up_sem, dinv_sem, fj_sem,
):
    core = meta[CORE]
    count = order_by_colour(meta, order)

    def up_copies(s):
        return face_copies(core, upper, order[s], upper_other, s, up_buf, s, up_sem)

    def dinv_copy(s):
        return pltpu.make_async_copy(dinv.at[order[s]], dinv_buf.at[s], dinv_sem.at[s])

    def fj_copies(s):
        return face_copies(core, fj_own, order[s], fj_other, order[s], fj_buf, s, fj_sem)

    @pl.loop(0, count)
    def _(s):
        for c in up_copies(s):
            c.start()

    @pl.loop(0, count)
    def _(s):
        dinv_copy(s).start()

    @pl.loop(0, count)
    def _(s):
        for c in fj_copies(s):
            c.start()

    new_out[...] = adj[...]
    send[:N_PART] = send_in[...]
    local[:N_EL] = local_in[...]
    local[N_EL] = jnp.zeros_like(local[N_EL])

    @pl.loop(0, count)
    def _(s):
        for c in up_copies(s):
            c.wait()
        e = order[s]
        total = jnp.zeros((R, N), jnp.float32)
        for f in range(N_FACE):
            ref = meta[REF + e * N_FACE + f]
            near = adj[jnp.minimum(ref, N_EL - 1)]
            far = unpack(recv[jnp.maximum(ref - N_EL, 0)])
            total += dot(jnp.where(ref < N_EL, near, far), up_buf[s, f])
        red[s] = (rhs[e] - total).astype(jnp.bfloat16)

    for half in range(2):

        @pl.when(count > 4 * half)
        def _():
            for s in range(4 * half, 4 * half + 4):

                @pl.when(s < count)
                def _():
                    dinv_copy(s).wait()

            for s in range(4 * half, 4 * half + 4):
                new[s] = dot(red[s], dinv_buf[s]).astype(jnp.bfloat16)

    @pl.loop(0, count)
    def _(s):
        for c in fj_copies(s):
            c.wait()
        e = order[s]
        new_out[e] = new[s]
        faces_of(meta, e, new[s], fj_buf, s, send, local)

    send_out[...] = send[:N_PART]
    local_out[...] = local[:N_EL]


def diagonal_kernel(rhs, new, local, djac, out):
    for i in range(rhs.shape[0]):
        out[i] = rhs[i] - local[i] - dot(new[i], djac[i])


def return_kernel(meta, base, recv, out, total):
    total[...] = jnp.zeros_like(total)

    @pl.loop(0, N_PART, unroll=4)
    def _(q):
        i = meta[SEND + q]
        total[i] += recv[q].astype(jnp.float32)

    for i in range(N_EL):
        out[i] = base[i] - unpack(total[i])


def shape(dims, dtype=jnp.bfloat16):
    return jax.ShapeDtypeStruct(dims, dtype)


def params(mib):
    return pltpu.CompilerParams(vmem_limit_bytes=mib * MIB)


def cost(blocks, moved):
    return pl.CostEstimate(flops=2 * blocks * R * N * N, bytes_accessed=moved, transcendentals=0)


BLOCK = 320 * 384 * 2
ROWS = (N_PART, 80, 128)
LOCAL = (N_EL, R, N)


def on_device(adjoint, adj_rhs, diag_inv, diag_jac, upper, face_jac, face_ref, send_list, colour):
    swap = [(0, 1), (1, 0)]
    core = lax.axis_index("rhs").astype(jnp.int32)
    meta = jnp.concatenate(
        [face_ref.reshape(-1), send_list.reshape(-1), colour, jnp.full((16,), core, jnp.int32)]
    )
    face_jac_other = lax.ppermute(face_jac, "rhs", swap)

    outgoing = pl.pallas_call(
        pack_kernel,
        out_shape=shape(ROWS),
        in_specs=[SMEM, VMEM],
        out_specs=VMEM,
        scratch_shapes=[pltpu.VMEM((N_EL, 80, 128), jnp.bfloat16)],
        compiler_params=params(8),
        cost_estimate=cost(0, 2 * MIB),
        name="pack_rows",
    )(meta, adjoint)
    incoming = lax.all_to_all(outgoing, "dom", split_axis=0, concat_axis=0, tiled=True)

    upper_zero = pl.pallas_call(
        select_kernel,
        out_shape=shape((C_MAX, 2, N, N)),
        in_specs=[SMEM, ANY],
        out_specs=ANY,
        scratch_shapes=[pltpu.SMEM((N_EL,), jnp.int32), pltpu.SemaphoreType.DMA((C_MAX,))],
        cost_estimate=cost(0, 32 * BLOCK),
        name="select_upper",
    )(meta, upper)
    upper_other = lax.ppermute(upper_zero, "rhs", swap)

    sent_early, local_early = pl.pallas_call(
        early_kernel,
        out_shape=(shape(ROWS), shape(LOCAL, jnp.float32)),
        in_specs=[SMEM, VMEM, ANY, ANY],
        out_specs=(VMEM, VMEM),
        scratch_shapes=[
            pltpu.SMEM((N_EL,), jnp.int32),
            pltpu.VMEM((N_PART + 1, 80, 128), jnp.bfloat16),
            pltpu.VMEM((N_EL + 1, R, N), jnp.float32),
            pltpu.VMEM((N_EL, N_FACE, N, N), jnp.bfloat16),
            pltpu.SemaphoreType.DMA((N_EL, 2)),
        ],
        compiler_params=params(28),
        cost_estimate=cost(64, 64 * BLOCK),
        name="early_faces",
    )(meta, adjoint, face_jac, face_jac_other)

    new, outbound, local = pl.pallas_call(
        sweep_kernel,
        out_shape=(shape(LOCAL), shape(ROWS), shape(LOCAL, jnp.float32)),
        in_specs=[SMEM, VMEM, VMEM, VMEM, VMEM, VMEM, ANY, ANY, ANY, ANY, ANY],
        out_specs=(VMEM, VMEM, VMEM),
        scratch_shapes=[
            pltpu.SMEM((N_EL,), jnp.int32),
            pltpu.VMEM((N_PART + 1, 80, 128), jnp.bfloat16),
            pltpu.VMEM((N_EL + 1, R, N), jnp.float32),
            pltpu.VMEM((C_MAX, R, N), jnp.bfloat16),
            pltpu.VMEM((C_MAX, R, N), jnp.bfloat16),
            pltpu.VMEM((C_MAX, N_FACE, N, N), jnp.bfloat16),
            pltpu.VMEM((C_MAX, N, N), jnp.bfloat16),
            pltpu.VMEM((C_MAX, N_FACE, N, N), jnp.bfloat16),
            pltpu.SemaphoreType.DMA((C_MAX, 2)),
            pltpu.SemaphoreType.DMA((C_MAX,)),
            pltpu.SemaphoreType.DMA((C_MAX, 2)),
        ],
        compiler_params=params(36),
        cost_estimate=cost(72, 72 * BLOCK),
        name="sweep",
    )(meta, adjoint, adj_rhs, incoming, sent_early, local_early, upper, upper_other, diag_inv,
      face_jac, face_jac_other)
    inbound = lax.all_to_all(outbound, "dom", split_axis=0, concat_axis=0, tiled=True)

    tile = pl.BlockSpec((4, R, N), lambda i: (i, 0, 0))
    base = pl.pallas_call(
        diagonal_kernel,
        out_shape=shape(LOCAL, jnp.float32),
        grid=(4,),
        in_specs=[tile, tile, tile, pl.BlockSpec((4, N, N), lambda i: (i, 0, 0))],
        out_specs=tile,
        compiler_params=params(12),
        cost_estimate=cost(16, 16 * BLOCK),
        name="diagonal",
    )(adj_rhs, new, local, diag_jac)

    residual = pl.pallas_call(
        return_kernel,
        out_shape=shape(LOCAL, jnp.float32),
        in_specs=[SMEM, VMEM, VMEM],
        out_specs=VMEM,
        scratch_shapes=[pltpu.VMEM((N_EL, 80, 128), jnp.float32)],
        compiler_params=params(8),
        cost_estimate=cost(0, 3 * MIB),
        name="return_sums",
    )(meta, base, inbound)
    return new, residual


def solution(mesh):
    in_specs = (
        P("dom", "rhs", None),
        P("dom", "rhs", None),
        P("dom", None, None),
        P("dom", None, None),
        P("dom", "rhs", None, None),
        P("dom", "rhs", None, None),
        P("dom", None),
        P("dom", None, None),
        P("dom"),
    )
    out_specs = (P("dom", "rhs", None), P("dom", "rhs", None))
    return jax.shard_map(
        on_device, mesh=mesh, in_specs=in_specs, out_specs=out_specs, check_vma=False
    )
```

```python
import jax
import jax.numpy as jnp
from jax import lax
from jax.experimental import pallas as pl
from jax.experimental.pallas import tpu as pltpu
from jax.sharding import PartitionSpec as P

N_EL, N_FACE, N_PART, C_MAX = 16, 4, 64, 8
N_JOB = C_MAX * N_FACE
R, N = 32, 320
MIB = 2**20
BF16, F32 = jnp.bfloat16, jnp.float32

SMEM = pl.BlockSpec(memory_space=pltpu.SMEM)
VMEM = pl.BlockSpec(memory_space=pltpu.VMEM)
HBM = pl.BlockSpec(memory_space=pltpu.HBM)
DMA = pltpu.SemaphoreType.DMA

ROWS = (N_PART, 80, 128)
LOCAL = (N_EL, R, N)

ELEM, JOB_S, JOB_BLOCK, JOB_AT, TABLE = 8, 32, 72, 112, 152


def dot(a, b):
    return jnp.dot(a, b, preferred_element_type=F32)


def pack(v):
    tail = jnp.concatenate([v[:16, 256:], v[16:, 256:]], axis=1)
    return jnp.concatenate([v[:, :128], v[:, 128:256], tail], axis=0)


def unpack(p):
    tail = jnp.concatenate([p[64:, :64], p[64:, 64:]], axis=0)
    return jnp.concatenate([p[:32], p[32:64], tail], axis=1)


def order_by_colour(colour, order):
    def place(e, carry):
        zeros, others = carry
        is_zero = colour[e] == 0
        order[jnp.where(is_zero, zeros, N_EL - 1 - others)] = e
        step = is_zero.astype(jnp.int32)
        return zeros + step, others + 1 - step

    return lax.fori_loop(0, N_EL, place, (jnp.int32(0), jnp.int32(0)))[0]


def pack_kernel(listed, adj, out, places, own, packed, rows, in_sem, out_sem):
    loads = [
        pltpu.make_async_copy(listed, places, in_sem.at[0]),
        pltpu.make_async_copy(adj, own, in_sem.at[1]),
    ]
    for c in loads:
        c.start()
    for c in loads:
        c.wait()
    for e in range(N_EL):
        packed[e] = pack(own[e])

    @pl.loop(0, 4)
    def _(g):
        for k in range(16):
            rows[16 * g + k] = packed[places[16 * g + k]]
        part = pl.ds(16 * g, 16)
        pltpu.make_async_copy(rows.at[part], out.at[part], out_sem).start()

    pltpu.make_async_copy(rows, out, out_sem).wait()


def landed(buf, sem):
    pltpu.make_async_copy(buf, buf, sem).wait()


def half(core_side):
    core = lax.axis_index("rhs")
    return 2 * core if core_side == 0 else 2 - 2 * core


def push_near(refs, adj, e, first, blocks):
    total = None
    for k in range(2):
        ref = refs[first + k, e]
        x = adj[jnp.minimum(ref, N_EL - 1)]
        product = dot(jnp.where(ref < N_EL, x, jnp.zeros_like(x)), blocks[k])
        total = product if total is None else total + product
    return total


def early_kernel(
    refs, colour, adj, rhs, upper, fj_own, fj_other, send_out, local_out, base_out,
    order, send, local, up_buf, buf, up_sem, sem,
):
    count = order_by_colour(colour, order)

    def up_copy(s):
        return pltpu.make_async_copy(upper.at[order[s]], up_buf.at[s], up_sem.at[s])

    @pl.loop(0, count)
    def _(s):
        up_copy(s).start()

    @pl.loop(count, N_EL)
    def _(s):
        e = order[s]
        for side, source in ((0, fj_own), (1, fj_other)):
            part = buf.at[s, pl.ds(half(side), 2)]
            pltpu.make_async_copy(source.at[e], part, sem.at[s]).start()

    send[...] = jnp.zeros_like(send)
    local[...] = jnp.zeros_like(local)

    @pl.loop(0, count)
    def _(s):
        up_copy(s).wait()
        e = order[s]
        base_out[s] = rhs[e] - push_near(refs, adj, e, half(0), up_buf[s])

    @pl.loop(count, N_EL)
    def _(s):
        landed(buf.at[s], sem.at[s])
        e = order[s]
        x = adj[e]
        for f in range(N_FACE):
            ref = refs[f, e]
            product = dot(x, buf[s, f])
            send[jnp.where(ref >= N_EL, ref - N_EL, N_PART)] = pack(product.astype(BF16))
            local[jnp.minimum(ref, N_EL)] += product

    send_out[...] = send[:N_PART]
    local_out[...] = local[:N_EL]


def near_kernel(
    refs, colour, adj, base_in, upper_other, base_out, adj_out, table, order, buf, sem
):
    count = order_by_colour(colour, order)

    def copy(s):
        return pltpu.make_async_copy(upper_other.at[order[s]], buf.at[s], sem.at[s])

    @pl.loop(0, count)
    def _(s):
        copy(s).start()

    adj_out[...] = adj[...]

    def add_jobs(first):
        def add(s, jobs):
            e = order[s]
            for k in range(2):
                ref = refs[first + k, e]

                @pl.when(ref >= N_EL)
                def _():
                    table[JOB_S + jobs] = s
                    table[JOB_BLOCK + jobs] = 2 * e + k
                    table[JOB_AT + jobs] = ref - N_EL

                jobs += (ref >= N_EL).astype(jnp.int32)
            return jobs

        return add

    own_jobs = lax.fori_loop(0, count, add_jobs(half(0)), jnp.int32(0))
    jobs = lax.fori_loop(0, count, add_jobs(half(1)), own_jobs)
    for k in range(3):
        table[JOB_S + jobs + k] = C_MAX
        table[JOB_BLOCK + jobs + k] = 0
        table[JOB_AT + jobs + k] = 0
    table[0] = count
    table[1] = own_jobs
    table[2] = jobs
    for s in range(C_MAX):
        table[ELEM + s] = order[s]

    @pl.loop(0, count)
    def _(s):
        copy(s).wait()
        base_out[s] = base_in[s] - push_near(refs, adj, order[s], half(1), buf[s])


def sweep_kernel(
    table, recv, base, upper, upper_other, dinv, fj_own, fj_other, new_in, send_in,
    new_out, send_out,
    start, total, new, row, up_buf, dinv_buf, fj_buf, up_sem, dinv_sem, fj_sem, base_sem, out_sem,
):
    del new_in, send_in
    count, own_jobs, jobs = table[0], table[1], table[2]
    groups = lax.div(jobs + 3, 4)

    def fetch(own, other, buf, sem):
        def copies(first, last, source):
            @pl.loop(first, last)
            def _(j):
                block = source.at[table[JOB_BLOCK + j]]
                pltpu.make_async_copy(block, buf.at[j], sem.at[lax.div(j, 4)]).start()

        copies(0, own_jobs, own)
        copies(own_jobs, 4 * groups, other)

    base_copy = pltpu.make_async_copy(base, start, base_sem)
    fetch(upper, upper_other, up_buf, up_sem)
    base_copy.start()
    for part in range(2):

        @pl.when(count > 4 * part)
        def _():
            for s in range(4 * part, 4 * part + 4):
                block = dinv.at[table[ELEM + s]]
                pltpu.make_async_copy(block, dinv_buf.at[s], dinv_sem.at[part]).start()

    fetch(fj_own, fj_other, fj_buf, fj_sem)
    total[...] = jnp.zeros_like(total)

    def in_groups(buf, sem, body):
        @pl.loop(0, groups)
        def _(g):
            landed(buf.at[pl.ds(4 * g, 4)], sem.at[g])
            body([4 * g + k for k in range(4)])

    def push(js):
        products = [dot(unpack(recv[table[JOB_AT + j]]), up_buf[j]) for j in js]
        for j, product in zip(js, products):
            total[table[JOB_S + j]] += product

    in_groups(up_buf, up_sem, push)
    base_copy.wait()
    for part in range(2):

        @pl.when(count > 4 * part)
        def _():
            landed(dinv_buf.at[pl.ds(4 * part, 4)], dinv_sem.at[part])
            reduced = [(start[s] - total[s]).astype(BF16) for s in range(4 * part, 4 * part + 4)]
            products = [dot(reduced[k], dinv_buf[4 * part + k]) for k in range(4)]
            for k in range(4):
                new[4 * part + k] = products[k].astype(BF16)

    def new_copy(s):
        return pltpu.make_async_copy(new.at[s], new_out.at[table[ELEM + s]], out_sem.at[0])

    def row_copy(j):
        return pltpu.make_async_copy(row.at[j], send_out.at[table[JOB_AT + j]], out_sem.at[1])

    @pl.loop(0, count)
    def _(s):
        new_copy(s).start()

    def spread(js):
        products = [dot(new[table[JOB_S + j]], fj_buf[j]) for j in js]
        for j, product in zip(js, products):
            row[j] = pack(product.astype(BF16))
        for j in js:

            @pl.when(j < jobs)
            def _():
                row_copy(j).start()

    in_groups(fj_buf, fj_sem, spread)

    @pl.loop(0, count)
    def _(s):
        new_copy(s).wait()

    @pl.loop(0, jobs)
    def _(j):
        row_copy(j).wait()


def diagonal_kernel(
    refs, colour, rhs, new, local_in, djac, fj_own, fj_other, out,
    order, local, djac_buf, fj_buf, local_sem, djac_sem, fj_sem,
):
    count = order_by_colour(colour, order)

    def djac_copy(g):
        part = pl.ds(4 * g, 4)
        return pltpu.make_async_copy(djac.at[part], djac_buf.at[part], djac_sem.at[g])

    local_copy = pltpu.make_async_copy(local_in, local.at[pl.ds(0, N_EL)], local_sem)
    local_copy.start()

    @pl.loop(0, count)
    def _(s):
        e = order[s]
        for side, source in ((0, fj_own), (1, fj_other)):
            part = fj_buf.at[s, pl.ds(half(side), 2)]
            pltpu.make_async_copy(source.at[e], part, fj_sem.at[s]).start()

    for g in range(4):
        djac_copy(g).start()
    local_copy.wait()
    local[N_EL] = jnp.zeros((R, N), F32)

    @pl.loop(0, count)
    def _(s):
        landed(fj_buf.at[s], fj_sem.at[s])
        e = order[s]
        products = [dot(new[e], fj_buf[s, f]) for f in range(N_FACE)]
        for f in range(N_FACE):
            local[jnp.minimum(refs[f, e], N_EL)] += products[f]

    @pl.loop(0, 4)
    def _(g):
        djac_copy(g).wait()
        for k in range(4):
            i = 4 * g + k
            out[i] = pack(rhs[i] - local[i] - dot(new[i], djac_buf[i]))


def return_kernel(listed, base, recv, out, places, base_buf, total, out_buf, in_sem, out_sem):
    places_copy = pltpu.make_async_copy(listed, places, in_sem.at[0])
    base_copy = pltpu.make_async_copy(base, base_buf, in_sem.at[1])
    places_copy.start()
    base_copy.start()
    total[...] = jnp.zeros_like(total)
    places_copy.wait()

    @pl.loop(0, N_PART, unroll=8)
    def _(q):
        total[places[q]] += recv[q].astype(F32)

    base_copy.wait()
    for g in range(4):
        for i in range(4 * g, 4 * g + 4):
            out_buf[i] = unpack(base_buf[i] - total[i])
        part = pl.ds(4 * g, 4)
        pltpu.make_async_copy(out_buf.at[part], out.at[part], out_sem).start()
    pltpu.make_async_copy(out_buf, out, out_sem).wait()


def call(kernel, out, in_specs, out_specs, scratch, mib, aliases=None):
    return pl.pallas_call(
        kernel,
        out_shape=out,
        in_specs=in_specs,
        out_specs=out_specs,
        scratch_shapes=scratch,
        input_output_aliases=aliases or {},
        compiler_params=pltpu.CompilerParams(vmem_limit_bytes=mib * MIB),
        cost_estimate=pl.CostEstimate(flops=0, bytes_accessed=0, transcendentals=0),
        name=kernel.__name__,
    )


def hbm(dims, dtype=BF16):
    return pltpu.HBM(dims, dtype)


def pin(a):
    return pltpu.with_memory_space_constraint(a, pltpu.HBM)


ORDER = pltpu.SMEM((N_EL,), jnp.int32)
LISTED = pltpu.SMEM((N_PART,), jnp.int32)
PACK_SCRATCH = [
    LISTED, pltpu.VMEM(LOCAL, BF16), pltpu.VMEM((N_EL, 80, 128), BF16), pltpu.VMEM(ROWS, BF16),
    DMA((2,)), DMA,
]
RETURN_SCRATCH = [
    LISTED, pltpu.VMEM((N_EL, 80, 128), F32), pltpu.VMEM((N_EL, 80, 128), F32), pltpu.VMEM(LOCAL, F32),
    DMA((2,)), DMA,
]
SWEEP_SCRATCH = [
    pltpu.VMEM((C_MAX, R, N), F32), pltpu.VMEM((C_MAX + 1, R, N), F32),
    pltpu.VMEM((C_MAX + 1, R, N), BF16), pltpu.VMEM((N_JOB, 80, 128), BF16),
    pltpu.VMEM((N_JOB, N, N), BF16), pltpu.VMEM((C_MAX, N, N), BF16), pltpu.VMEM((N_JOB, N, N), BF16),
    DMA((N_JOB // 4,)), DMA((2,)), DMA((N_JOB // 4,)), DMA, DMA((2,)),
]


def on_device(adjoint, adj_rhs, diag_inv, diag_jac, upper, face_jac, face_ref, send_list, colour):
    swap = [(0, 1), (1, 0)]
    blocks = (2 * N_EL, N, N)
    refs, listed, colour = pin(face_ref.T), pin(send_list.reshape(-1)), pin(colour)
    face_jac_other = lax.ppermute(face_jac, "rhs", swap)
    upper_other = lax.ppermute(upper, "rhs", swap)
    adj, rhs, fj, fj_other = pin(adjoint), pin(adj_rhs), pin(face_jac), pin(face_jac_other)

    outgoing = call(
        pack_kernel, hbm(ROWS), [HBM, HBM], HBM, PACK_SCRATCH,
        8,
    )(listed, adj)
    incoming = lax.all_to_all(outgoing, "dom", split_axis=0, concat_axis=0, tiled=True)

    sent, local, base_own = call(
        early_kernel, (hbm(ROWS), hbm(LOCAL, F32), hbm((C_MAX, R, N), F32)),
        [SMEM, SMEM, VMEM, VMEM, HBM, HBM, HBM], (VMEM, VMEM, VMEM),
        [ORDER, pltpu.VMEM((N_PART + 1, 80, 128), BF16), pltpu.VMEM((N_EL + 1, R, N), F32),
         pltpu.VMEM((C_MAX, 2, N, N), BF16), pltpu.VMEM((N_EL, N_FACE, N, N), BF16),
         DMA((C_MAX,)), DMA((N_EL,))],
        36,
    )(refs, colour, adj, rhs, pin(upper), fj, fj_other)

    base, kept, table = call(
        near_kernel, (hbm((C_MAX, R, N), F32), hbm(LOCAL), hbm((TABLE,), jnp.int32)),
        [SMEM, SMEM, VMEM, VMEM, HBM], (VMEM, VMEM, SMEM),
        [ORDER, pltpu.VMEM((C_MAX, 2, N, N), BF16), DMA((C_MAX,))],
        16,
    )(refs, colour, adj, pin(base_own), pin(upper_other))

    new, outbound = call(
        sweep_kernel, (hbm(LOCAL), hbm(ROWS)),
        [SMEM, VMEM, HBM, HBM, HBM, HBM, HBM, HBM, HBM, HBM], (HBM, HBM),
        SWEEP_SCRATCH,
        32, {8: 0, 9: 1},
    )(pin(table), incoming, pin(base), pin(upper.reshape(blocks)), pin(upper_other.reshape(blocks)),
      pin(diag_inv), pin(face_jac.reshape(blocks)), pin(face_jac_other.reshape(blocks)), pin(kept),
      pin(sent))
    inbound = lax.all_to_all(outbound, "dom", split_axis=0, concat_axis=0, tiled=True)

    own = call(
        diagonal_kernel, hbm((N_EL, 80, 128), F32), [SMEM, SMEM, VMEM, VMEM, HBM, HBM, HBM, HBM], VMEM,
        [ORDER, pltpu.VMEM((N_EL + 1, R, N), F32), pltpu.VMEM((N_EL, N, N), BF16),
         pltpu.VMEM((C_MAX, N_FACE, N, N), BF16), DMA, DMA((4,)), DMA((C_MAX,))],
        20,
    )(refs, colour, rhs, pin(new), pin(local), pin(diag_jac), fj, fj_other)

    residual = call(
        return_kernel, hbm(LOCAL, F32), [HBM, HBM, VMEM], HBM, RETURN_SCRATCH,
        8,
    )(listed, pin(own), inbound)
    return new, residual


def solution(mesh):
    in_specs = (
        P("dom", "rhs", None),
        P("dom", "rhs", None),
        P("dom", None, None),
        P("dom", None, None),
        P("dom", "rhs", None, None),
        P("dom", "rhs", None, None),
        P("dom", None),
        P("dom", None, None),
        P("dom"),
    )
    out_specs = (P("dom", "rhs", None), P("dom", "rhs", None))
    return jax.shard_map(
        on_device, mesh=mesh, in_specs=in_specs, out_specs=out_specs, check_vma=False
    )
```

```python
import jax
import jax.numpy as jnp
from jax import lax
from jax.experimental import pallas as pl
from jax.experimental.pallas import tpu as pltpu
from jax.sharding import PartitionSpec as P

N_EL, N_FACE, N_PART, C_MAX = 16, 4, 64, 8
N_JOB = C_MAX * N_FACE
R, N = 32, 320
MIB = 2**20
BF16, F32 = jnp.bfloat16, jnp.float32

SMEM = pl.BlockSpec(memory_space=pltpu.SMEM)
VMEM = pl.BlockSpec(memory_space=pltpu.VMEM)
HBM = pl.BlockSpec(memory_space=pltpu.HBM)
DMA = pltpu.SemaphoreType.DMA

ROWS = (N_PART, 80, 128)
LOCAL = (N_EL, R, N)

ELEM, JOB_S, JOB_BLOCK, JOB_AT = 8, 32, 72, 112
NEAR_S, NEAR_BLOCK, NEAR_AT, LIST, TABLE = 152, 176, 200, 224, 288


def dot(a, b):
    return jnp.dot(a, b, preferred_element_type=F32)


def pack(v):
    tail = jnp.concatenate([v[:16, 256:], v[16:, 256:]], axis=1)
    return jnp.concatenate([v[:, :128], v[:, 128:256], tail], axis=0)


def unpack(p):
    tail = jnp.concatenate([p[64:, :64], p[64:, 64:]], axis=0)
    return jnp.concatenate([p[:32], p[32:64], tail], axis=1)


def order_by_colour(colour, order):
    def place(e, carry):
        zeros, others = carry
        is_zero = colour[e] == 0
        order[jnp.where(is_zero, zeros, N_EL - 1 - others)] = e
        step = is_zero.astype(jnp.int32)
        return zeros + step, others + 1 - step

    return lax.fori_loop(0, N_EL, place, (jnp.int32(0), jnp.int32(0)))[0]


def pack_kernel(listed, adj, out, places, own, packed, rows, in_sem, out_sem):
    loads = [
        pltpu.make_async_copy(listed, places, in_sem.at[0]),
        pltpu.make_async_copy(adj, own, in_sem.at[1]),
    ]
    for c in loads:
        c.start()
    for c in loads:
        c.wait()
    for e in range(N_EL):
        packed[e] = pack(own[e])

    @pl.loop(0, 4)
    def _(g):
        for k in range(16):
            rows[16 * g + k] = packed[places[16 * g + k]]
        part = pl.ds(16 * g, 16)
        pltpu.make_async_copy(rows.at[part], out.at[part], out_sem).start()

    pltpu.make_async_copy(rows, out, out_sem).wait()


def landed(buf, sem):
    pltpu.make_async_copy(buf, buf, sem).wait()


def half(core_side):
    core = lax.axis_index("rhs")
    return 2 * core if core_side == 0 else 2 - 2 * core


def early_kernel(
    refs, colour, listed, adj, rhs, upper, fj_own, fj_other,
    send_out, local_out, base_out, adj_out, table,
    order, send, local, up_buf, buf, up_sem, sem,
):
    count = order_by_colour(colour, order)

    def up_copy(s):
        return pltpu.make_async_copy(upper.at[order[s]], up_buf.at[s], up_sem.at[s])

    @pl.loop(0, count)
    def _(s):
        up_copy(s).start()

    @pl.loop(count, N_EL)
    def _(s):
        e = order[s]
        for side, source in ((0, fj_own), (1, fj_other)):
            part = buf.at[s, pl.ds(half(side), 2)]
            pltpu.make_async_copy(source.at[e], part, sem.at[s]).start()

    send[...] = jnp.zeros_like(send)
    local[...] = jnp.zeros_like(local)
    adj_out[...] = adj[...]

    def list_faces(side, remote, places, start):
        def add(s, jobs):
            e = order[s]
            for k in range(2):
                ref = refs[half(side) + k, e]
                wanted = ref >= N_EL if remote else ref < N_EL

                @pl.when(wanted)
                def _():
                    table[places[0] + jobs] = s
                    table[places[1] + jobs] = 2 * e + k
                    table[places[2] + jobs] = ref - N_EL if remote else ref

                jobs += wanted.astype(jnp.int32)
            return jobs

        return lax.fori_loop(0, count, add, start)

    def close(places, jobs):
        for k in range(3):
            table[places[0] + jobs + k] = C_MAX
            table[places[1] + jobs + k] = 0
            table[places[2] + jobs + k] = 0

    far, near = (JOB_S, JOB_BLOCK, JOB_AT), (NEAR_S, NEAR_BLOCK, NEAR_AT)
    own_jobs = list_faces(0, True, far, jnp.int32(0))
    jobs = list_faces(1, True, far, own_jobs)
    near_jobs = list_faces(1, False, near, jnp.int32(0))
    close(far, jobs)
    close(near, near_jobs)
    for k, number in enumerate((count, own_jobs, jobs, near_jobs)):
        table[k] = number
    for s in range(C_MAX):
        table[ELEM + s] = order[s]

    @pl.loop(0, N_PART)
    def _(q):
        table[LIST + q] = listed[q]

    @pl.loop(0, count)
    def _(s):
        up_copy(s).wait()
        e = order[s]
        total = rhs[e]
        for k in range(2):
            ref = refs[half(0) + k, e]
            x = adj[jnp.minimum(ref, N_EL - 1)]
            total -= dot(jnp.where(ref < N_EL, x, jnp.zeros_like(x)), up_buf[s, k])
        base_out[s] = total

    @pl.loop(count, N_EL)
    def _(s):
        landed(buf.at[s], sem.at[s])
        e = order[s]
        x = adj[e]
        for f in range(N_FACE):
            ref = refs[f, e]
            product = dot(x, buf[s, f])
            send[jnp.where(ref >= N_EL, ref - N_EL, N_PART)] = pack(product.astype(BF16))
            local[jnp.minimum(ref, N_EL)] += product

    send_out[...] = send[:N_PART]
    local_out[...] = local[:N_EL]


def arrive(jobs, buf, sem, g):
    left = jobs - 4 * g
    for n in range(1, 5):

        @pl.when(left == n if n < 4 else left >= n)
        def _():
            landed(buf.at[pl.ds(4 * g, n)], sem.at[g])


def near_kernel(table, adj, base, upper_other, out, own, total, buf, in_sem, sem, out_sem):
    jobs = table[3]
    adj_copy = pltpu.make_async_copy(adj, own, in_sem.at[0])
    base_copy = pltpu.make_async_copy(base, total.at[pl.ds(0, C_MAX)], in_sem.at[1])

    @pl.loop(0, jobs)
    def _(j):
        block = upper_other.at[table[NEAR_BLOCK + j]]
        pltpu.make_async_copy(block, buf.at[j], sem.at[lax.div(j, 4)]).start()

    adj_copy.start()
    base_copy.start()
    adj_copy.wait()
    base_copy.wait()

    @pl.loop(0, lax.div(jobs + 3, 4))
    def _(g):
        arrive(jobs, buf, sem, g)
        js = [4 * g + k for k in range(4)]
        products = [dot(own[table[NEAR_AT + j]], buf[j]) for j in js]
        for j, product in zip(js, products):
            total[table[NEAR_S + j]] -= product

    out_copy = pltpu.make_async_copy(total.at[pl.ds(0, C_MAX)], out, out_sem)
    out_copy.start()
    out_copy.wait()


def sweep_kernel(
    table_in, recv, base, upper, upper_other, dinv, fj_own, fj_other, new_in, send_in,
    new_out, send_out,
    table, start, total, new, row, up_buf, dinv_buf, fj_buf, up_sem, dinv_sem, fj_sem, base_sem, out_sem,
):
    del new_in, send_in
    table_copy = pltpu.make_async_copy(table_in, table, out_sem.at[0])
    table_copy.start()
    total[...] = jnp.zeros_like(total)
    table_copy.wait()
    count, own_jobs, jobs = table[0], table[1], table[2]
    groups = lax.div(jobs + 3, 4)

    def fetch(own, other, buf, sem):
        def copies(first, last, source):
            @pl.loop(first, last)
            def _(j):
                block = source.at[table[JOB_BLOCK + j]]
                pltpu.make_async_copy(block, buf.at[j], sem.at[lax.div(j, 4)]).start()

        copies(0, own_jobs, own)
        copies(own_jobs, jobs, other)

    base_copy = pltpu.make_async_copy(base, start, base_sem)
    fetch(upper, upper_other, up_buf, up_sem)
    base_copy.start()
    for part in range(2):

        @pl.when(count > 4 * part)
        def _():
            for s in range(4 * part, 4 * part + 4):
                block = dinv.at[table[ELEM + s]]
                pltpu.make_async_copy(block, dinv_buf.at[s], dinv_sem.at[part]).start()

    fetch(fj_own, fj_other, fj_buf, fj_sem)

    def in_groups(buf, sem, body):
        @pl.loop(0, groups)
        def _(g):
            arrive(jobs, buf, sem, g)
            body([4 * g + k for k in range(4)])

    def push(js):
        products = [dot(unpack(recv[table[JOB_AT + j]]), up_buf[j]) for j in js]
        for j, product in zip(js, products):
            total[table[JOB_S + j]] += product

    in_groups(up_buf, up_sem, push)
    base_copy.wait()
    def solve(slots):
        reduced = [(start[s] - total[s]).astype(BF16) for s in slots]
        products = [dot(r, dinv_buf[s]) for r, s in zip(reduced, slots)]
        for s, product in zip(slots, products):
            new[s] = product.astype(BF16)

    landed(dinv_buf.at[pl.ds(0, 4)], dinv_sem.at[0])

    @pl.when(count <= 4)
    def _():
        solve(range(4))

    @pl.when(count > 4)
    def _():
        landed(dinv_buf.at[pl.ds(4, 4)], dinv_sem.at[1])
        solve(range(8))

    def new_copy(s):
        return pltpu.make_async_copy(new.at[s], new_out.at[table[ELEM + s]], out_sem.at[0])

    def row_copy(j):
        return pltpu.make_async_copy(row.at[j], send_out.at[table[JOB_AT + j]], out_sem.at[1])

    @pl.loop(0, count)
    def _(s):
        new_copy(s).start()

    def spread(js):
        products = [dot(new[table[JOB_S + j]], fj_buf[j]) for j in js]
        for j, product in zip(js, products):
            row[j] = pack(product.astype(BF16))
        for j in js:

            @pl.when(j < jobs)
            def _():
                row_copy(j).start()

    @pl.loop(0, lax.div(groups, 2))
    def _(h):
        for g in (2 * h, 2 * h + 1):
            arrive(jobs, fj_buf, fj_sem, g)
        spread([8 * h + k for k in range(8)])

    @pl.when(lax.rem(groups, 2) == 1)
    def _():
        arrive(jobs, fj_buf, fj_sem, groups - 1)
        spread([4 * (groups - 1) + k for k in range(4)])

    @pl.loop(0, count)
    def _(s):
        new_copy(s).wait()

    @pl.loop(0, jobs)
    def _(j):
        row_copy(j).wait()


def diagonal_kernel(
    refs, colour, rhs, new, local_in, djac, fj_own, fj_other, out,
    order, local, djac_buf, fj_buf, local_sem, djac_sem, fj_sem,
):
    count = order_by_colour(colour, order)

    def djac_copy(g):
        part = pl.ds(4 * g, 4)
        return pltpu.make_async_copy(djac.at[part], djac_buf.at[part], djac_sem.at[g])

    local_copy = pltpu.make_async_copy(local_in, local.at[pl.ds(0, N_EL)], local_sem)
    local_copy.start()

    @pl.loop(0, count)
    def _(s):
        e = order[s]
        for side, source in ((0, fj_own), (1, fj_other)):
            part = fj_buf.at[s, pl.ds(half(side), 2)]
            pltpu.make_async_copy(source.at[e], part, fj_sem.at[s]).start()

    for g in range(4):
        djac_copy(g).start()
    local_copy.wait()
    local[N_EL] = jnp.zeros((R, N), F32)

    @pl.loop(0, count)
    def _(s):
        landed(fj_buf.at[s], fj_sem.at[s])
        e = order[s]
        products = [dot(new[e], fj_buf[s, f]) for f in range(N_FACE)]
        for f in range(N_FACE):
            local[jnp.minimum(refs[f, e], N_EL)] += products[f]

    @pl.loop(0, 4)
    def _(g):
        djac_copy(g).wait()
        for k in range(4):
            i = 4 * g + k
            out[i] = pack(rhs[i] - local[i] - dot(new[i], djac_buf[i]))


def return_kernel(table_in, base, recv, out, table, base_buf, total, out_buf, in_sem, out_sem):
    table_copy = pltpu.make_async_copy(table_in, table, in_sem.at[0])
    base_copy = pltpu.make_async_copy(base, base_buf, in_sem.at[1])
    table_copy.start()
    base_copy.start()
    total[...] = jnp.zeros_like(total)
    table_copy.wait()

    @pl.loop(0, N_PART, unroll=8)
    def _(q):
        total[table[LIST + q]] += recv[q].astype(F32)

    base_copy.wait()
    for g in range(4):
        for i in range(4 * g, 4 * g + 4):
            out_buf[i] = unpack(base_buf[i] - total[i])
        part = pl.ds(4 * g, 4)
        pltpu.make_async_copy(out_buf.at[part], out.at[part], out_sem).start()
    pltpu.make_async_copy(out_buf, out, out_sem).wait()


def call(kernel, out, in_specs, out_specs, scratch, mib, aliases=None):
    return pl.pallas_call(
        kernel,
        out_shape=out,
        in_specs=in_specs,
        out_specs=out_specs,
        scratch_shapes=scratch,
        input_output_aliases=aliases or {},
        compiler_params=pltpu.CompilerParams(vmem_limit_bytes=mib * MIB),
        cost_estimate=pl.CostEstimate(flops=0, bytes_accessed=0, transcendentals=0),
        name=kernel.__name__,
    )


def hbm(dims, dtype=BF16):
    return pltpu.HBM(dims, dtype)


def pin(a):
    return pltpu.with_memory_space_constraint(a, pltpu.HBM)


ORDER = pltpu.SMEM((N_EL,), jnp.int32)
LISTED = pltpu.SMEM((N_PART,), jnp.int32)
PACK_SCRATCH = [
    LISTED, pltpu.VMEM(LOCAL, BF16), pltpu.VMEM((N_EL, 80, 128), BF16), pltpu.VMEM(ROWS, BF16),
    DMA((2,)), DMA,
]
RETURN_SCRATCH = [
    pltpu.SMEM((TABLE,), jnp.int32),
    pltpu.VMEM((N_EL, 80, 128), F32), pltpu.VMEM((N_EL, 80, 128), F32), pltpu.VMEM(LOCAL, F32), DMA((2,)), DMA,
]
SWEEP_SCRATCH = [
    pltpu.SMEM((TABLE,), jnp.int32),
    pltpu.VMEM((C_MAX, R, N), F32), pltpu.VMEM((C_MAX + 1, R, N), F32),
    pltpu.VMEM((C_MAX + 1, R, N), BF16), pltpu.VMEM((N_JOB, 80, 128), BF16),
    pltpu.VMEM((N_JOB, N, N), BF16), pltpu.VMEM((C_MAX, N, N), BF16), pltpu.VMEM((N_JOB, N, N), BF16),
    DMA((N_JOB // 4,)), DMA((2,)), DMA((N_JOB // 4,)), DMA, DMA((2,)),
]


def on_device(adjoint, adj_rhs, diag_inv, diag_jac, upper, face_jac, face_ref, send_list, colour):
    swap = [(0, 1), (1, 0)]
    blocks = (2 * N_EL, N, N)
    refs, listed, colour = pin(face_ref.T), pin(send_list.reshape(-1)), pin(colour)
    face_jac_other = lax.ppermute(face_jac, "rhs", swap)
    upper_other = lax.ppermute(upper, "rhs", swap)
    adj, rhs, fj, fj_other = pin(adjoint), pin(adj_rhs), pin(face_jac), pin(face_jac_other)

    outgoing = call(
        pack_kernel, hbm(ROWS), [HBM, HBM], HBM, PACK_SCRATCH,
        8,
    )(listed, adj)
    incoming = lax.all_to_all(outgoing, "dom", split_axis=0, concat_axis=0, tiled=True)

    sent, local, base_own, kept, table = call(
        early_kernel,
        (hbm(ROWS), hbm(LOCAL, F32), hbm((C_MAX, R, N), F32), hbm(LOCAL),
         jax.ShapeDtypeStruct((TABLE,), jnp.int32)),
        [SMEM, SMEM, SMEM, VMEM, VMEM, HBM, HBM, HBM], (VMEM, VMEM, VMEM, VMEM, SMEM),
        [ORDER, pltpu.VMEM((N_PART + 1, 80, 128), BF16), pltpu.VMEM((N_EL + 1, R, N), F32),
         pltpu.VMEM((C_MAX, 2, N, N), BF16), pltpu.VMEM((N_EL, N_FACE, N, N), BF16),
         DMA((C_MAX,)), DMA((N_EL,))],
        36,
    )(refs, colour, listed, adj, rhs, pin(upper), fj, fj_other)

    base = call(
        near_kernel, hbm((C_MAX, R, N), F32), [SMEM, HBM, HBM, HBM], HBM,
        [pltpu.VMEM(LOCAL, BF16), pltpu.VMEM((C_MAX + 1, R, N), F32),
         pltpu.VMEM((2 * C_MAX, N, N), BF16), DMA((2,)), DMA((C_MAX // 2,)), DMA],
        8,
    )(table, adj, pin(base_own), pin(upper_other.reshape(blocks)))

    new, outbound = call(
        sweep_kernel, (hbm(LOCAL), hbm(ROWS)),
        [VMEM, VMEM, HBM, HBM, HBM, HBM, HBM, HBM, HBM, HBM], (HBM, HBM),
        SWEEP_SCRATCH,
        32, {8: 0, 9: 1},
    )(table, incoming, pin(base), pin(upper.reshape(blocks)), pin(upper_other.reshape(blocks)),
      pin(diag_inv), pin(face_jac.reshape(blocks)), pin(face_jac_other.reshape(blocks)), pin(kept),
      pin(sent))
    inbound = lax.all_to_all(outbound, "dom", split_axis=0, concat_axis=0, tiled=True)

    own = call(
        diagonal_kernel, hbm((N_EL, 80, 128), F32), [SMEM, SMEM, VMEM, VMEM, HBM, HBM, HBM, HBM], VMEM,
        [ORDER, pltpu.VMEM((N_EL + 1, R, N), F32), pltpu.VMEM((N_EL, N, N), BF16),
         pltpu.VMEM((C_MAX, N_FACE, N, N), BF16), DMA, DMA((4,)), DMA((C_MAX,))],
        20,
    )(refs, colour, rhs, pin(new), pin(local), pin(diag_jac), fj, fj_other)

    residual = call(
        return_kernel, hbm(LOCAL, F32), [VMEM, HBM, VMEM], HBM, RETURN_SCRATCH,
        8,
    )(table, pin(own), inbound)
    return new, residual


def solution(mesh):
    in_specs = (
        P("dom", "rhs", None),
        P("dom", "rhs", None),
        P("dom", None, None),
        P("dom", None, None),
        P("dom", "rhs", None, None),
        P("dom", "rhs", None, None),
        P("dom", None),
        P("dom", None, None),
        P("dom"),
    )
    out_specs = (P("dom", "rhs", None), P("dom", "rhs", None))
    return jax.shard_map(
        on_device, mesh=mesh, in_specs=in_specs, out_specs=out_specs, check_vma=False
    )
```

```python
import jax
import jax.numpy as jnp
from jax import lax
from jax.experimental import pallas as pl
from jax.experimental.pallas import tpu as pltpu
from jax.sharding import PartitionSpec as P

N_EL, N_FACE, N_PART, C_MAX = 16, 4, 64, 8
N_JOB = C_MAX * N_FACE
N_FIRST = 8
R, N = 32, 320
MIB = 2**20
BF16, F32 = jnp.bfloat16, jnp.float32

SMEM = pl.BlockSpec(memory_space=pltpu.SMEM)
VMEM = pl.BlockSpec(memory_space=pltpu.VMEM)
HBM = pl.BlockSpec(memory_space=pltpu.HBM)
DMA = pltpu.SemaphoreType.DMA

ROWS = (N_PART, 80, 128)
LOCAL = (N_EL, R, N)

ELEM, JOB_S, JOB_BLOCK, JOB_AT = 8, 32, 72, 112
NEAR_S, NEAR_BLOCK, NEAR_AT, LIST, TABLE = 152, 176, 200, 224, 288


def dot(a, b):
    return jnp.dot(a, b, preferred_element_type=F32)


def pack(v):
    tail = jnp.concatenate([v[:16, 256:], v[16:, 256:]], axis=1)
    return jnp.concatenate([v[:, :128], v[:, 128:256], tail], axis=0)


def unpack(p):
    tail = jnp.concatenate([p[64:, :64], p[64:, 64:]], axis=0)
    return jnp.concatenate([p[:32], p[32:64], tail], axis=1)


def order_by_colour(colour, order):
    def place(e, carry):
        zeros, others = carry
        is_zero = colour[e] == 0
        order[jnp.where(is_zero, zeros, N_EL - 1 - others)] = e
        step = is_zero.astype(jnp.int32)
        return zeros + step, others + 1 - step

    return lax.fori_loop(0, N_EL, place, (jnp.int32(0), jnp.int32(0)))[0]


def pack_kernel(listed, adj, out, places, own, packed, rows, in_sem, out_sem):
    loads = [
        pltpu.make_async_copy(listed, places, in_sem.at[0]),
        pltpu.make_async_copy(adj, own, in_sem.at[1]),
    ]
    for c in loads:
        c.start()
    for c in loads:
        c.wait()
    for e in range(N_EL):
        packed[e] = pack(own[e])

    @pl.loop(0, 4)
    def _(g):
        for k in range(16):
            rows[16 * g + k] = packed[places[16 * g + k]]
        part = pl.ds(16 * g, 16)
        pltpu.make_async_copy(rows.at[part], out.at[part], out_sem).start()

    pltpu.make_async_copy(rows, out, out_sem).wait()


def landed(buf, sem):
    pltpu.make_async_copy(buf, buf, sem).wait()


def half(core_side):
    core = lax.axis_index("rhs")
    return 2 * core if core_side == 0 else 2 - 2 * core


def early_kernel(
    refs, colour, listed, adj, rhs, upper, fj_own, fj_other,
    send_out, local_out, base_out, adj_out, table, first_out,
    order, send, local, up_buf, buf, up_sem, sem, first_sem,
):
    count = order_by_colour(colour, order)

    def up_copy(s):
        return pltpu.make_async_copy(upper.at[order[s]], up_buf.at[s], up_sem.at[s])

    @pl.loop(0, count)
    def _(s):
        up_copy(s).start()

    @pl.loop(count, N_EL)
    def _(s):
        e = order[s]
        for side, source in ((0, fj_own), (1, fj_other)):
            part = buf.at[s, pl.ds(half(side), 2)]
            pltpu.make_async_copy(source.at[e], part, sem.at[s]).start()

    send[...] = jnp.zeros_like(send)
    local[...] = jnp.zeros_like(local)
    adj_out[...] = adj[...]

    def list_faces(side, remote, places, start):
        def add(s, jobs):
            e = order[s]
            for k in range(2):
                ref = refs[half(side) + k, e]
                wanted = ref >= N_EL if remote else ref < N_EL

                @pl.when(wanted)
                def _():
                    table[places[0] + jobs] = s
                    table[places[1] + jobs] = 2 * e + k
                    table[places[2] + jobs] = ref - N_EL if remote else ref

                jobs += wanted.astype(jnp.int32)
            return jobs

        return lax.fori_loop(0, count, add, start)

    def close(places, jobs):
        for k in range(3):
            table[places[0] + jobs + k] = C_MAX
            table[places[1] + jobs + k] = 0
            table[places[2] + jobs + k] = 0

    far, near = (JOB_S, JOB_BLOCK, JOB_AT), (NEAR_S, NEAR_BLOCK, NEAR_AT)
    own_jobs = list_faces(0, True, far, jnp.int32(0))
    jobs = list_faces(1, True, far, own_jobs)
    near_jobs = list_faces(1, False, near, jnp.int32(0))
    close(far, jobs)
    close(near, near_jobs)
    ready = jnp.minimum(lax.div(own_jobs, 4), N_FIRST // 4) * 4
    for k, number in enumerate((count, own_jobs, jobs, near_jobs, ready)):
        table[k] = number

    def first_copy(j):
        block = table[JOB_BLOCK + j]
        source = upper.at[lax.div(block, 2), lax.rem(block, 2)]
        return pltpu.make_async_copy(source, first_out.at[j], first_sem)

    @pl.loop(0, ready)
    def _(j):
        first_copy(j).start()

    for s in range(C_MAX):
        table[ELEM + s] = order[s]

    @pl.loop(0, N_PART)
    def _(q):
        table[LIST + q] = listed[q]

    @pl.loop(0, count)
    def _(s):
        up_copy(s).wait()
        e = order[s]
        total = rhs[e]
        for k in range(2):
            ref = refs[half(0) + k, e]
            x = adj[jnp.minimum(ref, N_EL - 1)]
            total -= dot(jnp.where(ref < N_EL, x, jnp.zeros_like(x)), up_buf[s, k])
        base_out[s] = total

    @pl.loop(count, N_EL)
    def _(s):
        landed(buf.at[s], sem.at[s])
        e = order[s]
        x = adj[e]
        for f in range(N_FACE):
            ref = refs[f, e]
            product = dot(x, buf[s, f])
            send[jnp.where(ref >= N_EL, ref - N_EL, N_PART)] = pack(product.astype(BF16))
            local[jnp.minimum(ref, N_EL)] += product

    send_out[...] = send[:N_PART]
    local_out[...] = local[:N_EL]

    @pl.loop(0, ready)
    def _(j):
        first_copy(j).wait()


def arrive(jobs, buf, sem, g):
    left = jobs - 4 * g
    for n in range(1, 5):

        @pl.when(left == n if n < 4 else left >= n)
        def _():
            landed(buf.at[pl.ds(4 * g, n)], sem.at[g])


def near_kernel(table, adj, base, upper_other, out, own, total, buf, in_sem, sem, out_sem):
    jobs = table[3]
    adj_copy = pltpu.make_async_copy(adj, own, in_sem.at[0])
    base_copy = pltpu.make_async_copy(base, total.at[pl.ds(0, C_MAX)], in_sem.at[1])

    @pl.loop(0, jobs)
    def _(j):
        block = upper_other.at[table[NEAR_BLOCK + j]]
        pltpu.make_async_copy(block, buf.at[j], sem.at[lax.div(j, 4)]).start()

    adj_copy.start()
    base_copy.start()
    adj_copy.wait()
    base_copy.wait()

    @pl.loop(0, lax.div(jobs + 3, 4))
    def _(g):
        arrive(jobs, buf, sem, g)
        js = [4 * g + k for k in range(4)]
        products = [dot(own[table[NEAR_AT + j]], buf[j]) for j in js]
        for j, product in zip(js, products):
            total[table[NEAR_S + j]] -= product

    out_copy = pltpu.make_async_copy(total.at[pl.ds(0, C_MAX)], out, out_sem)
    out_copy.start()
    out_copy.wait()


def sweep_kernel(
    table_in, first, recv, base, upper, upper_other, dinv, fj_own, fj_other, new_in, send_in,
    new_out, send_out,
    table, start, total, new, row, up_buf, dinv_buf, fj_buf, up_sem, dinv_sem, fj_sem, base_sem, out_sem,
):
    del new_in, send_in
    table_copy = pltpu.make_async_copy(table_in, table, out_sem.at[0])
    table_copy.start()
    total[...] = jnp.zeros_like(total)
    table_copy.wait()
    count, own_jobs, jobs, ready = table[0], table[1], table[2], table[4]
    groups = lax.div(jobs + 3, 4)

    def fetch(start_at, own, other, buf, sem):
        def copies(first, last, source):
            @pl.loop(first, last)
            def _(j):
                block = source.at[table[JOB_BLOCK + j]]
                pltpu.make_async_copy(block, buf.at[j], sem.at[lax.div(j, 4)]).start()

        copies(start_at, own_jobs, own)
        copies(own_jobs, jobs, other)

    base_copy = pltpu.make_async_copy(base, start, base_sem)
    fetch(ready, upper, upper_other, up_buf, up_sem)
    base_copy.start()
    for part in range(2):

        @pl.when(count > 4 * part)
        def _():
            for s in range(4 * part, 4 * part + 4):
                block = dinv.at[table[ELEM + s]]
                pltpu.make_async_copy(block, dinv_buf.at[s], dinv_sem.at[part]).start()

    fetch(0, fj_own, fj_other, fj_buf, fj_sem)

    def push(js, blocks):
        products = [dot(unpack(recv[table[JOB_AT + j]]), blocks[j]) for j in js]
        for j, product in zip(js, products):
            total[table[JOB_S + j]] += product

    @pl.loop(0, lax.div(ready, 4))
    def _(g):
        push([4 * g + k for k in range(4)], first)

    @pl.loop(lax.div(ready, 4), groups)
    def _(g):
        arrive(jobs, up_buf, up_sem, g)
        push([4 * g + k for k in range(4)], up_buf)

    base_copy.wait()
    def solve(slots):
        reduced = [(start[s] - total[s]).astype(BF16) for s in slots]
        products = [dot(r, dinv_buf[s]) for r, s in zip(reduced, slots)]
        for s, product in zip(slots, products):
            new[s] = product.astype(BF16)

    landed(dinv_buf.at[pl.ds(0, 4)], dinv_sem.at[0])

    @pl.when(count <= 4)
    def _():
        solve(range(4))

    @pl.when(count > 4)
    def _():
        landed(dinv_buf.at[pl.ds(4, 4)], dinv_sem.at[1])
        solve(range(8))

    def new_copy(s):
        return pltpu.make_async_copy(new.at[s], new_out.at[table[ELEM + s]], out_sem.at[0])

    def row_copy(j):
        return pltpu.make_async_copy(row.at[j], send_out.at[table[JOB_AT + j]], out_sem.at[1])

    @pl.loop(0, count)
    def _(s):
        new_copy(s).start()

    def spread(js):
        products = [dot(new[table[JOB_S + j]], fj_buf[j]) for j in js]
        for j, product in zip(js, products):
            row[j] = pack(product.astype(BF16))
        for j in js:

            @pl.when(j < jobs)
            def _():
                row_copy(j).start()

    @pl.loop(0, lax.div(groups, 2))
    def _(h):
        for g in (2 * h, 2 * h + 1):
            arrive(jobs, fj_buf, fj_sem, g)
        spread([8 * h + k for k in range(8)])

    @pl.when(lax.rem(groups, 2) == 1)
    def _():
        arrive(jobs, fj_buf, fj_sem, groups - 1)
        spread([4 * (groups - 1) + k for k in range(4)])

    @pl.loop(0, count)
    def _(s):
        new_copy(s).wait()

    @pl.loop(0, jobs)
    def _(j):
        row_copy(j).wait()


def diagonal_kernel(
    refs, colour, rhs, new, local_in, djac, fj_own, fj_other, out,
    order, local, djac_buf, fj_buf, local_sem, djac_sem, fj_sem,
):
    count = order_by_colour(colour, order)

    def djac_copy(g):
        part = pl.ds(4 * g, 4)
        return pltpu.make_async_copy(djac.at[part], djac_buf.at[part], djac_sem.at[g])

    local_copy = pltpu.make_async_copy(local_in, local.at[pl.ds(0, N_EL)], local_sem)
    local_copy.start()

    @pl.loop(0, count)
    def _(s):
        e = order[s]
        for side, source in ((0, fj_own), (1, fj_other)):
            part = fj_buf.at[s, pl.ds(half(side), 2)]
            pltpu.make_async_copy(source.at[e], part, fj_sem.at[s]).start()

    for g in range(4):
        djac_copy(g).start()
    local_copy.wait()
    local[N_EL] = jnp.zeros((R, N), F32)

    @pl.loop(0, count)
    def _(s):
        landed(fj_buf.at[s], fj_sem.at[s])
        e = order[s]
        products = [dot(new[e], fj_buf[s, f]) for f in range(N_FACE)]
        for f in range(N_FACE):
            local[jnp.minimum(refs[f, e], N_EL)] += products[f]

    @pl.loop(0, 4)
    def _(g):
        djac_copy(g).wait()
        for k in range(4):
            i = 4 * g + k
            out[i] = pack(rhs[i] - local[i] - dot(new[i], djac_buf[i]))


def return_kernel(table_in, base, recv, out, table, total, out_buf, in_sem, out_sem):
    table_copy = pltpu.make_async_copy(table_in, table, in_sem)
    table_copy.start()
    total[...] = base[...]
    table_copy.wait()

    @pl.loop(0, N_PART, unroll=8)
    def _(q):
        total[table[LIST + q]] -= recv[q].astype(F32)

    for g in range(4):
        for i in range(4 * g, 4 * g + 4):
            out_buf[i] = unpack(total[i])
        part = pl.ds(4 * g, 4)
        pltpu.make_async_copy(out_buf.at[part], out.at[part], out_sem).start()
    pltpu.make_async_copy(out_buf, out, out_sem).wait()


def call(kernel, out, in_specs, out_specs, scratch, mib, aliases=None):
    return pl.pallas_call(
        kernel,
        out_shape=out,
        in_specs=in_specs,
        out_specs=out_specs,
        scratch_shapes=scratch,
        input_output_aliases=aliases or {},
        compiler_params=pltpu.CompilerParams(vmem_limit_bytes=mib * MIB),
        cost_estimate=pl.CostEstimate(flops=0, bytes_accessed=0, transcendentals=0),
        name=kernel.__name__,
    )


def hbm(dims, dtype=BF16):
    return pltpu.HBM(dims, dtype)


def pin(a):
    return pltpu.with_memory_space_constraint(a, pltpu.HBM)


ORDER = pltpu.SMEM((N_EL,), jnp.int32)
LISTED = pltpu.SMEM((N_PART,), jnp.int32)
PACK_SCRATCH = [
    LISTED, pltpu.VMEM(LOCAL, BF16), pltpu.VMEM((N_EL, 80, 128), BF16), pltpu.VMEM(ROWS, BF16),
    DMA((2,)), DMA,
]
RETURN_SCRATCH = [
    pltpu.SMEM((TABLE,), jnp.int32), pltpu.VMEM((N_EL, 80, 128), F32), pltpu.VMEM(LOCAL, F32), DMA, DMA,
]
SWEEP_SCRATCH = [
    pltpu.SMEM((TABLE,), jnp.int32),
    pltpu.VMEM((C_MAX, R, N), F32), pltpu.VMEM((C_MAX + 1, R, N), F32),
    pltpu.VMEM((C_MAX + 1, R, N), BF16), pltpu.VMEM((N_JOB, 80, 128), BF16),
    pltpu.VMEM((N_JOB, N, N), BF16), pltpu.VMEM((C_MAX, N, N), BF16), pltpu.VMEM((N_JOB, N, N), BF16),
    DMA((N_JOB // 4,)), DMA((2,)), DMA((N_JOB // 4,)), DMA, DMA((2,)),
]


def on_device(adjoint, adj_rhs, diag_inv, diag_jac, upper, face_jac, face_ref, send_list, colour):
    swap = [(0, 1), (1, 0)]
    blocks = (2 * N_EL, N, N)
    refs, listed, colour = pin(face_ref.T), pin(send_list.reshape(-1)), pin(colour)
    face_jac_other = lax.ppermute(face_jac, "rhs", swap)
    upper_other = lax.ppermute(upper, "rhs", swap)
    adj, rhs, fj, fj_other = pin(adjoint), pin(adj_rhs), pin(face_jac), pin(face_jac_other)

    outgoing = call(
        pack_kernel, hbm(ROWS), [HBM, HBM], HBM, PACK_SCRATCH,
        8,
    )(listed, adj)
    incoming = lax.all_to_all(outgoing, "dom", split_axis=0, concat_axis=0, tiled=True)

    sent, local, base_own, kept, table, first = call(
        early_kernel,
        (hbm(ROWS), hbm(LOCAL, F32), hbm((C_MAX, R, N), F32), hbm(LOCAL),
         jax.ShapeDtypeStruct((TABLE,), jnp.int32), jax.ShapeDtypeStruct((N_FIRST, N, N), BF16)),
        [SMEM, SMEM, SMEM, VMEM, VMEM, HBM, HBM, HBM], (VMEM, VMEM, VMEM, VMEM, SMEM, VMEM),
        [ORDER, pltpu.VMEM((N_PART + 1, 80, 128), BF16), pltpu.VMEM((N_EL + 1, R, N), F32),
         pltpu.VMEM((C_MAX, 2, N, N), BF16), pltpu.VMEM((N_EL, N_FACE, N, N), BF16),
         DMA((C_MAX,)), DMA((N_EL,)), DMA],
        36,
    )(refs, colour, listed, adj, rhs, pin(upper), fj, fj_other)

    base = call(
        near_kernel, hbm((C_MAX, R, N), F32), [SMEM, HBM, HBM, HBM], HBM,
        [pltpu.VMEM(LOCAL, BF16), pltpu.VMEM((C_MAX + 1, R, N), F32),
         pltpu.VMEM((2 * C_MAX, N, N), BF16), DMA((2,)), DMA((C_MAX // 2,)), DMA],
        8,
    )(table, adj, pin(base_own), pin(upper_other.reshape(blocks)))

    new, outbound = call(
        sweep_kernel, (hbm(LOCAL), hbm(ROWS)),
        [VMEM, VMEM, VMEM, HBM, HBM, HBM, HBM, HBM, HBM, HBM, HBM], (HBM, HBM),
        SWEEP_SCRATCH,
        32, {9: 0, 10: 1},
    )(table, first, incoming, pin(base), pin(upper.reshape(blocks)), pin(upper_other.reshape(blocks)),
      pin(diag_inv), pin(face_jac.reshape(blocks)), pin(face_jac_other.reshape(blocks)), pin(kept),
      pin(sent))
    inbound = lax.all_to_all(outbound, "dom", split_axis=0, concat_axis=0, tiled=True)

    own = call(
        diagonal_kernel, jax.ShapeDtypeStruct((N_EL, 80, 128), F32), [SMEM, SMEM, VMEM, VMEM, HBM, HBM, HBM, HBM], VMEM,
        [ORDER, pltpu.VMEM((N_EL + 1, R, N), F32), pltpu.VMEM((N_EL, N, N), BF16),
         pltpu.VMEM((C_MAX, N_FACE, N, N), BF16), DMA, DMA((4,)), DMA((C_MAX,))],
        20,
    )(refs, colour, rhs, pin(new), pin(local), pin(diag_jac), fj, fj_other)

    residual = call(
        return_kernel, hbm(LOCAL, F32), [VMEM, VMEM, VMEM], HBM, RETURN_SCRATCH,
        8,
    )(table, own, inbound)
    return new, residual


def solution(mesh):
    in_specs = (
        P("dom", "rhs", None),
        P("dom", "rhs", None),
        P("dom", None, None),
        P("dom", None, None),
        P("dom", "rhs", None, None),
        P("dom", "rhs", None, None),
        P("dom", None),
        P("dom", None, None),
        P("dom"),
    )
    out_specs = (P("dom", "rhs", None), P("dom", "rhs", None))
    return jax.shard_map(
        on_device, mesh=mesh, in_specs=in_specs, out_specs=out_specs, check_vma=False
    )
```

```python
import jax
import jax.numpy as jnp
from jax import lax
from jax.experimental import pallas as pl
from jax.experimental.pallas import tpu as pltpu
from jax.sharding import PartitionSpec as P

N_EL, N_FACE, N_PART, C_MAX = 16, 4, 64, 8
N_JOB = C_MAX * N_FACE
N_FIRST = 8
R, N = 32, 320
MIB = 2**20
BF16, F32 = jnp.bfloat16, jnp.float32

SMEM = pl.BlockSpec(memory_space=pltpu.SMEM)
VMEM = pl.BlockSpec(memory_space=pltpu.VMEM)
HBM = pl.BlockSpec(memory_space=pltpu.HBM)
DMA = pltpu.SemaphoreType.DMA

ROWS = (N_PART, 80, 128)
LOCAL = (N_EL, R, N)

ELEM, JOB_S, JOB_BLOCK, JOB_AT = 8, 32, 72, 112
NEAR_S, NEAR_BLOCK, NEAR_AT, LIST, TABLE = 152, 176, 200, 224, 288


def dot(a, b):
    return jnp.dot(a, b, preferred_element_type=F32)


def pack(v):
    tail = jnp.concatenate([v[:16, 256:], v[16:, 256:]], axis=1)
    return jnp.concatenate([v[:, :128], v[:, 128:256], tail], axis=0)


def unpack(p):
    tail = jnp.concatenate([p[64:, :64], p[64:, 64:]], axis=0)
    return jnp.concatenate([p[:32], p[32:64], tail], axis=1)


def order_by_colour(colour, order):
    def place(e, carry):
        zeros, others = carry
        is_zero = colour[e] == 0
        order[jnp.where(is_zero, zeros, N_EL - 1 - others)] = e
        step = is_zero.astype(jnp.int32)
        return zeros + step, others + 1 - step

    return lax.fori_loop(0, N_EL, place, (jnp.int32(0), jnp.int32(0)))[0]


def pack_kernel(listed, adj, out, places, own, packed, rows, in_sem, out_sem):
    loads = [
        pltpu.make_async_copy(listed, places, in_sem.at[0]),
        pltpu.make_async_copy(adj, own, in_sem.at[1]),
    ]
    for c in loads:
        c.start()
    for c in loads:
        c.wait()
    for e in range(N_EL):
        packed[e] = pack(own[e])

    @pl.loop(0, 4)
    def _(g):
        for k in range(16):
            rows[16 * g + k] = packed[places[16 * g + k]]
        part = pl.ds(16 * g, 16)
        pltpu.make_async_copy(rows.at[part], out.at[part], out_sem).start()

    pltpu.make_async_copy(rows, out, out_sem).wait()


def landed(buf, sem):
    pltpu.make_async_copy(buf, buf, sem).wait()


def half(core_side):
    core = lax.axis_index("rhs")
    return 2 * core if core_side == 0 else 2 - 2 * core


def early_kernel(
    refs, colour, listed, adj, rhs, upper, fj_own, fj_other,
    send_out, local_out, base_out, adj_out, table, first_out,
    order, send, local, up_buf, buf, up_sem, sem, first_sem,
):
    count = order_by_colour(colour, order)

    def up_copy(s):
        return pltpu.make_async_copy(upper.at[order[s]], up_buf.at[s], up_sem.at[s])

    @pl.loop(0, count)
    def _(s):
        up_copy(s).start()

    @pl.loop(count, N_EL)
    def _(s):
        e = order[s]
        for side, source in ((0, fj_own), (1, fj_other)):
            part = buf.at[s, pl.ds(half(side), 2)]
            pltpu.make_async_copy(source.at[e], part, sem.at[s]).start()

    send[...] = jnp.zeros_like(send)
    local[...] = jnp.zeros_like(local)
    adj_out[...] = adj[...]

    def list_faces(side, remote, places, start):
        def add(s, jobs):
            e = order[s]
            for k in range(2):
                ref = refs[half(side) + k, e]
                wanted = ref >= N_EL if remote else ref < N_EL

                @pl.when(wanted)
                def _():
                    table[places[0] + jobs] = s
                    table[places[1] + jobs] = 2 * e + k
                    table[places[2] + jobs] = ref - N_EL if remote else ref

                jobs += wanted.astype(jnp.int32)
            return jobs

        return lax.fori_loop(0, count, add, start)

    def close(places, jobs):
        for k in range(3):
            table[places[0] + jobs + k] = C_MAX
            table[places[1] + jobs + k] = 0
            table[places[2] + jobs + k] = 0

    far, near = (JOB_S, JOB_BLOCK, JOB_AT), (NEAR_S, NEAR_BLOCK, NEAR_AT)
    own_jobs = list_faces(0, True, far, jnp.int32(0))
    jobs = list_faces(1, True, far, own_jobs)
    near_jobs = list_faces(1, False, near, jnp.int32(0))
    close(far, jobs)
    close(near, near_jobs)
    ready = jnp.minimum(own_jobs, N_FIRST)
    for k, number in enumerate((count, own_jobs, jobs, near_jobs, ready)):
        table[k] = number

    def first_copy(j):
        block = table[JOB_BLOCK + j]
        source = upper.at[lax.div(block, 2), lax.rem(block, 2)]
        return pltpu.make_async_copy(source, first_out.at[j], first_sem)

    @pl.loop(0, ready)
    def _(j):
        first_copy(j).start()

    for s in range(C_MAX):
        table[ELEM + s] = order[s]

    @pl.loop(0, N_PART)
    def _(q):
        table[LIST + q] = listed[q]

    @pl.loop(0, count)
    def _(s):
        up_copy(s).wait()
        e = order[s]
        total = rhs[e]
        for k in range(2):
            ref = refs[half(0) + k, e]
            x = adj[jnp.minimum(ref, N_EL - 1)]
            total -= dot(jnp.where(ref < N_EL, x, jnp.zeros_like(x)), up_buf[s, k])
        base_out[s] = total

    @pl.loop(count, N_EL)
    def _(s):
        landed(buf.at[s], sem.at[s])
        e = order[s]
        x = adj[e]
        for f in range(N_FACE):
            ref = refs[f, e]
            product = dot(x, buf[s, f])
            send[jnp.where(ref >= N_EL, ref - N_EL, N_PART)] = pack(product.astype(BF16))
            local[jnp.minimum(ref, N_EL)] += product

    send_out[...] = send[:N_PART]
    local_out[...] = local[:N_EL]

    @pl.loop(0, ready)
    def _(j):
        first_copy(j).wait()


def arrive(jobs, buf, sem, g):
    left = jobs - 4 * g
    for n in range(1, 5):

        @pl.when(left == n if n < 4 else left >= n)
        def _():
            landed(buf.at[pl.ds(4 * g, n)], sem.at[g])


def near_kernel(table_in, adj, base, upper_other, out, table, own, total, buf, in_sem, sem, out_sem):
    table_copy = pltpu.make_async_copy(table_in, table, out_sem)
    table_copy.start()
    table_copy.wait()
    jobs = table[3]
    adj_copy = pltpu.make_async_copy(adj, own, in_sem.at[0])
    base_copy = pltpu.make_async_copy(base, total.at[pl.ds(0, C_MAX)], in_sem.at[1])

    @pl.loop(0, jobs)
    def _(j):
        block = upper_other.at[table[NEAR_BLOCK + j]]
        pltpu.make_async_copy(block, buf.at[j], sem.at[lax.div(j, 4)]).start()

    adj_copy.start()
    base_copy.start()
    adj_copy.wait()
    base_copy.wait()

    @pl.loop(0, lax.div(jobs + 3, 4))
    def _(g):
        arrive(jobs, buf, sem, g)
        js = [4 * g + k for k in range(4)]
        products = [dot(own[table[NEAR_AT + j]], buf[j]) for j in js]
        for j, product in zip(js, products):
            total[table[NEAR_S + j]] -= product

    out_copy = pltpu.make_async_copy(total.at[pl.ds(0, C_MAX)], out, out_sem)
    out_copy.start()
    out_copy.wait()


def sweep_kernel(
    table_in, first, recv, base, upper, upper_other, dinv, fj_own, fj_other, new_in, send_in,
    new_out, send_out,
    table, start, total, new, row, up_buf, dinv_buf, fj_buf, up_sem, dinv_sem, fj_sem, base_sem, out_sem,
):
    del new_in, send_in
    table_copy = pltpu.make_async_copy(table_in, table, out_sem.at[0])
    table_copy.start()
    total[...] = jnp.zeros_like(total)
    table_copy.wait()
    count, own_jobs, jobs, ready = table[0], table[1], table[2], table[4]
    groups = lax.div(jobs + 3, 4)

    def fetch(start_at, own, other, buf, sem):
        def copies(first, last, source):
            @pl.loop(first, last)
            def _(j):
                block = source.at[table[JOB_BLOCK + j]]
                at = j - start_at
                pltpu.make_async_copy(block, buf.at[at], sem.at[lax.div(at, 4)]).start()

        copies(start_at, own_jobs, own)
        copies(own_jobs, jobs, other)

    base_copy = pltpu.make_async_copy(base, start, base_sem)
    fetch(ready, upper, upper_other, up_buf, up_sem)
    base_copy.start()
    for part in range(2):

        @pl.when(count > 4 * part)
        def _():
            for s in range(4 * part, 4 * part + 4):
                block = dinv.at[table[ELEM + s]]
                pltpu.make_async_copy(block, dinv_buf.at[s], dinv_sem.at[part]).start()

    fetch(0, fj_own, fj_other, fj_buf, fj_sem)

    def push(js, rows, blocks):
        products = [dot(unpack(recv[table[JOB_AT + j]]), block) for j, block in zip(js, blocks)]
        for at, product in zip(rows, products):
            total[at] += product

    @pl.loop(0, lax.div(ready + 3, 4))
    def _(g):
        js = [4 * g + k for k in range(4)]
        rows = [jnp.where(j < ready, table[JOB_S + j], C_MAX) for j in js]
        push(js, rows, [first[j] for j in js])

    @pl.loop(0, lax.div(jobs - ready + 3, 4))
    def _(g):
        arrive(jobs - ready, up_buf, up_sem, g)
        js = [ready + 4 * g + k for k in range(4)]
        push(js, [table[JOB_S + j] for j in js], [up_buf[4 * g + k] for k in range(4)])

    base_copy.wait()
    def solve(slots):
        reduced = [(start[s] - total[s]).astype(BF16) for s in slots]
        products = [dot(r, dinv_buf[s]) for r, s in zip(reduced, slots)]
        for s, product in zip(slots, products):
            new[s] = product.astype(BF16)

    landed(dinv_buf.at[pl.ds(0, 4)], dinv_sem.at[0])

    @pl.when(count <= 4)
    def _():
        solve(range(4))

    @pl.when(count > 4)
    def _():
        landed(dinv_buf.at[pl.ds(4, 4)], dinv_sem.at[1])
        solve(range(8))

    def new_copy(s):
        return pltpu.make_async_copy(new.at[s], new_out.at[table[ELEM + s]], out_sem.at[0])

    def row_copy(j):
        return pltpu.make_async_copy(row.at[j], send_out.at[table[JOB_AT + j]], out_sem.at[1])

    @pl.loop(0, count)
    def _(s):
        new_copy(s).start()

    def spread(js):
        products = [dot(new[table[JOB_S + j]], fj_buf[j]) for j in js]
        for j, product in zip(js, products):
            row[j] = pack(product.astype(BF16))
        for j in js:

            @pl.when(j < jobs)
            def _():
                row_copy(j).start()

    @pl.loop(0, lax.div(groups, 2))
    def _(h):
        for g in (2 * h, 2 * h + 1):
            arrive(jobs, fj_buf, fj_sem, g)
        spread([8 * h + k for k in range(8)])

    @pl.when(lax.rem(groups, 2) == 1)
    def _():
        arrive(jobs, fj_buf, fj_sem, groups - 1)
        spread([4 * (groups - 1) + k for k in range(4)])

    @pl.loop(0, count)
    def _(s):
        new_copy(s).wait()

    @pl.loop(0, jobs)
    def _(j):
        row_copy(j).wait()


def diagonal_kernel(
    refs, colour, rhs, new, local_in, djac, fj_own, fj_other, out,
    order, local, djac_buf, fj_buf, local_sem, djac_sem, fj_sem,
):
    count = order_by_colour(colour, order)

    def djac_copy(g):
        part = pl.ds(4 * g, 4)
        return pltpu.make_async_copy(djac.at[part], djac_buf.at[part], djac_sem.at[g])

    local_copy = pltpu.make_async_copy(local_in, local.at[pl.ds(0, N_EL)], local_sem)
    local_copy.start()

    @pl.loop(0, count)
    def _(s):
        e = order[s]
        for side, source in ((0, fj_own), (1, fj_other)):
            part = fj_buf.at[s, pl.ds(half(side), 2)]
            pltpu.make_async_copy(source.at[e], part, fj_sem.at[s]).start()

    for g in range(4):
        djac_copy(g).start()
    local_copy.wait()
    local[N_EL] = jnp.zeros((R, N), F32)

    @pl.loop(0, count)
    def _(s):
        landed(fj_buf.at[s], fj_sem.at[s])
        e = order[s]
        products = [dot(new[e], fj_buf[s, f]) for f in range(N_FACE)]
        for f in range(N_FACE):
            local[jnp.minimum(refs[f, e], N_EL)] += products[f]

    @pl.loop(0, 4)
    def _(g):
        djac_copy(g).wait()
        for k in range(4):
            i = 4 * g + k
            out[i] = pack(rhs[i] - local[i] - dot(new[i], djac_buf[i]))


def return_kernel(table_in, base, recv, out, table, total, out_buf, in_sem, out_sem):
    table_copy = pltpu.make_async_copy(table_in, table, in_sem)
    table_copy.start()
    total[...] = base[...]
    table_copy.wait()

    @pl.loop(0, N_PART, unroll=8)
    def _(q):
        total[table[LIST + q]] -= recv[q].astype(F32)

    for g in range(4):
        for i in range(4 * g, 4 * g + 4):
            out_buf[i] = unpack(total[i])
        part = pl.ds(4 * g, 4)
        pltpu.make_async_copy(out_buf.at[part], out.at[part], out_sem).start()
    pltpu.make_async_copy(out_buf, out, out_sem).wait()


def call(kernel, out, in_specs, out_specs, scratch, mib, aliases=None):
    return pl.pallas_call(
        kernel,
        out_shape=out,
        in_specs=in_specs,
        out_specs=out_specs,
        scratch_shapes=scratch,
        input_output_aliases=aliases or {},
        compiler_params=pltpu.CompilerParams(vmem_limit_bytes=mib * MIB),
        cost_estimate=pl.CostEstimate(flops=0, bytes_accessed=0, transcendentals=0),
        name=kernel.__name__,
    )


def hbm(dims, dtype=BF16):
    return pltpu.HBM(dims, dtype)


def pin(a):
    return pltpu.with_memory_space_constraint(a, pltpu.HBM)


ORDER = pltpu.SMEM((N_EL,), jnp.int32)
LISTED = pltpu.SMEM((N_PART,), jnp.int32)
PACK_SCRATCH = [
    LISTED, pltpu.VMEM(LOCAL, BF16), pltpu.VMEM((N_EL, 80, 128), BF16), pltpu.VMEM(ROWS, BF16),
    DMA((2,)), DMA,
]
RETURN_SCRATCH = [
    pltpu.SMEM((TABLE,), jnp.int32), pltpu.VMEM((N_EL, 80, 128), F32), pltpu.VMEM(LOCAL, F32), DMA, DMA,
]
SWEEP_SCRATCH = [
    pltpu.SMEM((TABLE,), jnp.int32),
    pltpu.VMEM((C_MAX, R, N), F32), pltpu.VMEM((C_MAX + 1, R, N), F32),
    pltpu.VMEM((C_MAX + 1, R, N), BF16), pltpu.VMEM((N_JOB, 80, 128), BF16),
    pltpu.VMEM((N_JOB, N, N), BF16), pltpu.VMEM((C_MAX, N, N), BF16), pltpu.VMEM((N_JOB, N, N), BF16),
    DMA((N_JOB // 4,)), DMA((2,)), DMA((N_JOB // 4,)), DMA, DMA((2,)),
]


def on_device(adjoint, adj_rhs, diag_inv, diag_jac, upper, face_jac, face_ref, send_list, colour):
    swap = [(0, 1), (1, 0)]
    blocks = (2 * N_EL, N, N)
    refs, listed, colour = pin(face_ref.T), pin(send_list.reshape(-1)), pin(colour)
    face_jac_other = lax.ppermute(face_jac, "rhs", swap)
    upper_other = lax.ppermute(upper, "rhs", swap)
    adj, rhs, fj, fj_other = pin(adjoint), pin(adj_rhs), pin(face_jac), pin(face_jac_other)

    outgoing = call(
        pack_kernel, hbm(ROWS), [HBM, HBM], HBM, PACK_SCRATCH,
        8,
    )(listed, adj)
    incoming = lax.all_to_all(outgoing, "dom", split_axis=0, concat_axis=0, tiled=True)

    sent, local, base_own, kept, table, first = call(
        early_kernel,
        (hbm(ROWS), hbm(LOCAL, F32), hbm((C_MAX, R, N), F32), hbm(LOCAL),
         jax.ShapeDtypeStruct((TABLE,), jnp.int32), jax.ShapeDtypeStruct((N_FIRST, N, N), BF16)),
        [SMEM, SMEM, SMEM, VMEM, VMEM, HBM, HBM, HBM], (VMEM, VMEM, VMEM, VMEM, SMEM, VMEM),
        [ORDER, pltpu.VMEM((N_PART + 1, 80, 128), BF16), pltpu.VMEM((N_EL + 1, R, N), F32),
         pltpu.VMEM((C_MAX, 2, N, N), BF16), pltpu.VMEM((N_EL, N_FACE, N, N), BF16),
         DMA((C_MAX,)), DMA((N_EL,)), DMA],
        36,
    )(refs, colour, listed, adj, rhs, pin(upper), fj, fj_other)

    base = call(
        near_kernel, hbm((C_MAX, R, N), F32), [VMEM, HBM, HBM, HBM], HBM,
        [pltpu.SMEM((TABLE,), jnp.int32), pltpu.VMEM(LOCAL, BF16), pltpu.VMEM((C_MAX + 1, R, N), F32),
         pltpu.VMEM((2 * C_MAX, N, N), BF16), DMA((2,)), DMA((C_MAX // 2,)), DMA],
        8,
    )(table, adj, pin(base_own), pin(upper_other.reshape(blocks)))

    new, outbound = call(
        sweep_kernel, (hbm(LOCAL), hbm(ROWS)),
        [VMEM, VMEM, VMEM, HBM, HBM, HBM, HBM, HBM, HBM, HBM, HBM], (HBM, HBM),
        SWEEP_SCRATCH,
        32, {9: 0, 10: 1},
    )(table, first, incoming, pin(base), pin(upper.reshape(blocks)), pin(upper_other.reshape(blocks)),
      pin(diag_inv), pin(face_jac.reshape(blocks)), pin(face_jac_other.reshape(blocks)), pin(kept),
      pin(sent))
    inbound = lax.all_to_all(outbound, "dom", split_axis=0, concat_axis=0, tiled=True)

    own = call(
        diagonal_kernel, jax.ShapeDtypeStruct((N_EL, 80, 128), F32), [SMEM, SMEM, VMEM, VMEM, HBM, HBM, HBM, HBM], VMEM,
        [ORDER, pltpu.VMEM((N_EL + 1, R, N), F32), pltpu.VMEM((N_EL, N, N), BF16),
         pltpu.VMEM((C_MAX, N_FACE, N, N), BF16), DMA, DMA((4,)), DMA((C_MAX,))],
        20,
    )(refs, colour, rhs, pin(new), pin(local), pin(diag_jac), fj, fj_other)

    residual = call(
        return_kernel, hbm(LOCAL, F32), [VMEM, VMEM, VMEM], HBM, RETURN_SCRATCH,
        8,
    )(table, own, inbound)
    return new, residual


def solution(mesh):
    in_specs = (
        P("dom", "rhs", None),
        P("dom", "rhs", None),
        P("dom", None, None),
        P("dom", None, None),
        P("dom", "rhs", None, None),
        P("dom", "rhs", None, None),
        P("dom", None),
        P("dom", None, None),
        P("dom"),
    )
    out_specs = (P("dom", "rhs", None), P("dom", "rhs", None))
    return jax.shard_map(
        on_device, mesh=mesh, in_specs=in_specs, out_specs=out_specs, check_vma=False
    )
```
